32 devices in a mesh: expert: 2 (over x), dp: 16 (over z, y, core).
Axes of the slice: x: 2, y: 2, z: 4, core: 2. Of those that a mesh axis runs over, the one named last changes fastest.
Arguments:
- tokens_in: bfloat16 [2048, 7168], P('dp', 'expert'), may hold values from -6 to 6
- out_grad: bfloat16 [2048, 7168], P('dp', 'expert'), may hold values from -0.59765625 to 0.59765625
- expert_ids: int32 [2048, 8], P('dp'), may hold values from 0 to 15, all different within a row; in each aligned block of 128 rows (0 to 127, 128 to 255, ...) at most 80 rows name the same one
- route_weight: bfloat16 [2048, 8], P('dp'), may hold values from 0.019897461 to 0.5
- gate_weight: bfloat16 [16, 7168, 1024], P('dp', 'expert'), may hold values from -0.0625 to 0.0625
- up_weight: bfloat16 [16, 7168, 1024], P('dp', 'expert'), may hold values from -0.0625 to 0.0625
- down_weight: bfloat16 [16, 1024, 7168], P('dp', None, 'expert'), may hold values from -0.1875 to 0.1875
Outputs:
- input_grad: bfloat16 [2048, 7168], P('dp', 'expert')
- weight_grad: bfloat16 [2048, 8], P('dp')
- gate_grad: bfloat16 [16, 7168, 1024], P('dp', 'expert')
- up_grad: bfloat16 [16, 7168, 1024], P('dp', 'expert')
- down_grad: bfloat16 [16, 1024, 7168], P('dp', None, 'expert')
The draws below stay inside these ranges and needn't reach their ends.
Inputs may be any that keep to these rules, and one draw needn't show every extreme that they name: `expert_ids`: each token names 8 different experts. Among the tokens of one dp index (aligned blocks of 128 tokens) no expert is named more than 80 times, a bound that some block reaches.
All inputs are finite; a program needn't handle non-finite values.
Results may differ from the reference program's by a relative error of at most 0.024.
Values may be sent and summed in bfloat16 or wider, within the bound.
No kernel may reach another device: no remote copies, remote signals or barrier semaphores. Data moves between devices by JAX's collectives and lax.ppermute only.
A program may use at most 192 MiB of HBM per device.

```python
import math
import jax
import jax.numpy as jnp
import numpy as np
from jax import lax

D = 7168
FF = 1024
TOP = 8
TOK_DEV = 128
EXPERTS = 16
TOKENS = 2048
CAP = 80
N_EXPERT = 2
N_DP = 16


def level_of(key, extent, split, low, top_value):
    def one(dim, shards_of):
        steps = jax.random.uniform(jax.random.fold_in(jax.random.fold_in(key, 6), dim), (shards_of,), jnp.float32, low / len(split), top_value / len(split))
        return jnp.repeat(jnp.exp(steps), extent[dim] // shards_of).reshape((-1,) + (1,) * (len(extent) - dim - 1))

    factor_of = one(*split[0])
    for cut in split[1:]:
        factor_of = factor_of * one(*cut)
    return factor_of


def deal_out(key, own, number, rows, amount, top, bound, slope):
    order = jax.random.permutation(key, amount)
    packed, ordinary = portions_of(amount, rows * top, bound, slope, True), portions_of(amount, rows * top, bound, slope, False)
    places = jnp.arange(amount)

    def named(lengths, offset_by):
        used = int((lengths > 0).sum())
        fixed = max(1, used // 4)
        passed = fixed + (places - fixed + offset_by * (used - fixed)) % max(1, amount - fixed)
        return jnp.zeros((amount,), jnp.int32).at[order[jnp.where(places < fixed, places, passed)]].set(jnp.asarray(lengths, jnp.int32))

    lengths = jnp.where(number % 4 == 0, named(packed, number // 4), named(ordinary, number - number // 4 - 1))
    mixed = jax.random.permutation(jax.random.fold_in(own, 3), amount)
    donor, sink = mixed[0:amount // 2 * 2:2], mixed[1:amount // 2 * 2:2]
    slack = jnp.minimum(lengths[donor] - 1, bound - lengths[sink]) // 2
    slack = jnp.where((donor == order[0]) | (sink == order[0]) | (lengths[sink] == 0), 0, jnp.maximum(slack, 0))
    passed = jax.random.randint(jax.random.fold_in(own, 4), (amount // 2,), 0, 1 << 20) % (slack + 1)
    lengths = lengths.at[donor].add(-passed).at[sink].add(passed)
    items = jnp.searchsorted(jnp.cumsum(lengths), jnp.arange(rows * top), side="right").astype(jnp.int32)
    grid = items.reshape(top, rows).T
    grid = grid[jax.random.permutation(jax.random.fold_in(own, 1), rows)]
    offset_by = jax.random.randint(jax.random.fold_in(own, 2), (rows, 1), 0, top)
    return jnp.take_along_axis(grid, (jnp.arange(top)[None, :] + offset_by) % top, axis=1)


def portions_of(number_of, total, limit, lean, full):
    weights = [(1 << 20) // math.isqrt(grade ** lean) + 1 for grade in range(1, number_of + 1)]
    largest = limit if full else min(limit, max(-(-total // number_of), total * weights[0] // sum(weights)))
    least = 1 if total - largest >= number_of - 1 else 0
    holding, rest = [largest] + [least] * (number_of - 1), total - largest - least * (number_of - 1)
    while rest > 0:
        free = [i for i in range(1, number_of) if holding[i] < largest] or [i for i in range(1, number_of) if holding[i] < limit]
        pool, left = sum([weights[i] for i in free]), rest
        for i in free:
            more = min(limit - holding[i], max(1, left * weights[i] // pool), rest)
            holding[i] = holding[i] + more
            rest = rest - more
    return np.array(holding)


def normal_values(stream_key, extent, deviation, bound, cuts=(), kind=jnp.bfloat16):
    drawn = deviation * jax.random.normal(stream_key, extent, jnp.float32)
    if cuts:
        drawn = drawn * level_of(stream_key, extent, cuts, -0.22, 0.18)
    return jnp.clip(drawn, -bound, bound).astype(kind)


def setup_inputs(seed: int = 0) -> dict:
    seeds = jax.random.split(jax.random.key(seed), 8)
    tokens_in = normal_values(seeds[0], (TOKENS, D), 1.0, 6.0, ((0, 16), (1, 2)))
    out_grad = normal_values(seeds[1], (TOKENS, D), 0.1, 0.59765625, ((0, 16), (1, 2)))
    expert_ids_keys = jax.random.split(jax.random.fold_in(seeds[2], 1), TOKENS // TOK_DEV)
    expert_ids_turns = jax.random.permutation(jax.random.fold_in(seeds[2], 3), TOKENS // TOK_DEV)
    expert_ids = jax.vmap(lambda own, number: deal_out(jax.random.fold_in(seeds[2], 2), own, number, TOK_DEV, EXPERTS, TOP, CAP, 2))(expert_ids_keys, expert_ids_turns).reshape((TOKENS, TOP))
    route_weight = jnp.clip(jnp.exp(math.log(0.5) - 3.224016 * jax.random.uniform(seeds[3], (TOKENS, TOP), jnp.float32) ** level_of(seeds[3], (TOKENS, TOP), ((0, 16),), -0.2, 0.2)), 0.019897461, 0.5).astype(jnp.bfloat16)
    gate_weight = normal_values(seeds[4], (EXPERTS, D, FF), D ** -0.5, 0.0625, ((0, 16), (1, 2)))
    up_weight = normal_values(seeds[5], (EXPERTS, D, FF), D ** -0.5, 0.0625, ((0, 16), (1, 2)))
    down_weight = normal_values(seeds[6], (EXPERTS, FF, D), FF ** -0.5, 0.1875, ((0, 16), (2, 2)))
    return dict(tokens_in=tokens_in, out_grad=out_grad, expert_ids=expert_ids, route_weight=route_weight, gate_weight=gate_weight, up_weight=up_weight, down_weight=down_weight)


def slice_sums(rows, matrix):
    row_count = rows.shape[0]
    slice_width = D // N_EXPERT
    left = rows.astype(jnp.float32).reshape(row_count, N_EXPERT, slice_width)
    right = matrix.astype(jnp.float32).reshape(N_EXPERT, slice_width, FF)
    pieces = jnp.einsum("rnd,ndf->rnf", left, right, precision=lax.Precision.HIGHEST).astype(jnp.bfloat16)
    pieces = lax.optimization_barrier(pieces)
    return jnp.sum(pieces.astype(jnp.float32), axis=1)


def reference(tokens_in, out_grad, expert_ids, route_weight, gate_weight, up_weight, down_weight):
    routes_all = TOKENS * TOP
    expert_rows = N_DP * CAP
    flat_experts = expert_ids.reshape(-1).astype(jnp.int32)
    onehot = (flat_experts[:, None] == jnp.arange(EXPERTS, dtype=jnp.int32)[None, :]).astype(jnp.int32)
    counted = jnp.cumsum(onehot.reshape(N_DP, TOK_DEV * TOP, EXPERTS), axis=1).reshape(routes_all, EXPERTS)
    route_rank = jnp.sum(onehot * (counted - 1), axis=1).astype(jnp.int32)
    source = (jnp.arange(routes_all, dtype=jnp.int32) // (TOK_DEV * TOP)).astype(jnp.int32)
    slot_index = (flat_experts * expert_rows + source * CAP + route_rank).astype(jnp.int32)
    route_of_slot = jnp.full((EXPERTS * expert_rows,), routes_all, jnp.int32).at[slot_index].set(jnp.arange(routes_all, dtype=jnp.int32))
    token_of_slot = jnp.where(route_of_slot < routes_all, route_of_slot // TOP, TOKENS).astype(jnp.int32)
    tokens_padded = jnp.concatenate([tokens_in, jnp.zeros((1, D), tokens_in.dtype)], axis=0)
    grads_padded = jnp.concatenate([out_grad, jnp.zeros((1, D), out_grad.dtype)], axis=0)
    weight_padded = jnp.concatenate([route_weight.reshape(-1), jnp.zeros((1,), route_weight.dtype)], axis=0)

    def expert_step(carried, inputs):
        input_total, weight_total = carried
        gate_mat, up_mat, down_mat, token_index, route_index = inputs
        rows_in = tokens_padded[token_index]
        rows_back = grads_padded[token_index]
        route_scale = weight_padded[route_index].astype(jnp.float32)
        gate_act = slice_sums(rows_in, gate_mat)
        up_act = slice_sums(rows_in, up_mat)
        back_act = slice_sums(rows_back, down_mat.T)
        gate_sigmoid = jax.nn.sigmoid(gate_act)
        gate_silu = gate_act * gate_sigmoid
        hidden = (gate_silu * up_act).astype(jnp.bfloat16)
        weight_dot = jnp.sum(hidden.astype(jnp.float32) * back_act, axis=1).astype(jnp.bfloat16)
        hidden_grad = route_scale[:, None] * back_act
        gate_delta = (hidden_grad * up_act * gate_sigmoid * (1.0 + gate_act * (1.0 - gate_sigmoid))).astype(jnp.bfloat16)
        up_delta = (hidden_grad * gate_silu).astype(jnp.bfloat16)
        gate_piece = jnp.dot(rows_in.T, gate_delta, preferred_element_type=jnp.float32).astype(jnp.bfloat16)
        up_piece = jnp.dot(rows_in.T, up_delta, preferred_element_type=jnp.float32).astype(jnp.bfloat16)
        scaled = (route_scale[:, None] * rows_back.astype(jnp.float32)).astype(jnp.bfloat16)
        down_piece = jnp.dot(hidden.T, scaled, preferred_element_type=jnp.float32).astype(jnp.bfloat16)
        route_term = (jnp.dot(gate_delta, gate_mat.T, preferred_element_type=jnp.float32) + jnp.dot(up_delta, up_mat.T, preferred_element_type=jnp.float32)).astype(jnp.bfloat16)
        input_total = input_total.at[token_index].add(route_term.astype(jnp.float32))
        weight_total = weight_total.at[route_index].set(weight_dot)
        return (input_total, weight_total), (gate_piece, up_piece, down_piece)

    initial = (jnp.zeros((TOKENS + 1, D), jnp.float32), jnp.zeros((routes_all + 1,), jnp.bfloat16))
    token_table = token_of_slot.reshape(EXPERTS, expert_rows)
    route_table = route_of_slot.reshape(EXPERTS, expert_rows)
    (input_total, weight_total), (gate_grad, up_grad, down_grad) = lax.scan(expert_step, initial, (gate_weight, up_weight, down_weight, token_table, route_table))
    input_grad = input_total[:TOKENS].astype(jnp.bfloat16)
    weight_grad = weight_total[:routes_all].reshape(TOKENS, TOP)
    return input_grad, weight_grad, gate_grad, up_grad, down_grad
```

```python
import functools

import jax
import jax.numpy as jnp
from jax import lax
from jax.experimental import pallas as pl
from jax.experimental.pallas import tpu as pltpu
from jax.sharding import PartitionSpec as P

BF16 = jnp.bfloat16
F32 = jnp.float32
LANES = 128
VMEM_LIMIT = 44 * 1024 * 1024


def split_dp(size):
    core = 2 if size % 2 == 0 else 1
    chips = size // core
    inner = 1
    while chips % (inner * 2) == 0 and (inner * 2) * (inner * 2) <= chips:
        inner *= 2
    return chips // inner, inner, core


def tile_of(size, most):
    best = LANES
    for tile in range(LANES, most + 1, LANES):
        if size % tile == 0:
            best = tile
    return best


def dot(a, b, dims=((1,), (0,))):
    return lax.dot_general(a, b, (dims, ((), ())), preferred_element_type=F32)


def cost(flops, moved):
    return pl.CostEstimate(flops=flops, bytes_accessed=moved, transcendentals=0)


def gate(x, after):
    return x if after is None or (isinstance(after, tuple) and not after) else lax.optimization_barrier((x, after))[0]


def whole(shape):
    zeros = (0,) * len(shape)
    return pl.BlockSpec(shape, lambda *_: zeros)


def choose(pick_t, block_ref, cols, slots):
    pick = jnp.transpose(pick_t.astype(F32))[:slots].astype(BF16)
    return dot(pick, block_ref[:, cols]).astype(BF16)


def fore_kernel(n, slots, top, width, step_cols, *refs):
    me_ref, block_refs = refs[0], refs[1 : 1 + n]
    gate_ref, up_ref = refs[1 + n : 3 + n]
    rows_ref, part_ref, pick_ref, scale_ref = refs[-4:]

    @pl.when(pl.program_id(0) == 0)
    def _():
        me = me_ref[0].astype(F32)
        count = block_refs[0].shape[0]
        lower = (
            lax.broadcasted_iota(jnp.int32, (count, count), 1)
            < lax.broadcasted_iota(jnp.int32, (count, count), 0)
        ).astype(BF16)
        lane = lax.broadcasted_iota(jnp.int32, (count, LANES), 1).astype(F32)
        for b in range(n):
            meta = block_refs[b][:, width : width + LANES].astype(F32)
            hit = (meta[:, :top] == me).astype(F32)
            chosen = jnp.max(hit, axis=1, keepdims=True)
            weight = jnp.sum(hit * meta[:, top : 2 * top], axis=1, keepdims=True)
            chosen = jnp.broadcast_to(chosen, (count, LANES))
            order = dot(lower, chosen.astype(BF16))
            pick_t = jnp.where((order == lane) & (chosen > 0.5), 1.0, 0.0)
            pick_ref[b] = pick_t.astype(BF16)
            pick = jnp.transpose(pick_t)[:slots].astype(BF16)
            at = pl.ds(b * slots, slots)
            scale_ref[at, :] = dot(pick, jnp.broadcast_to(weight, (count, LANES)).astype(BF16))
            for left in range(0, width, step_cols):
                cols = slice(left, left + step_cols)
                rows_ref[at, cols] = dot(pick, block_refs[b][:, cols]).astype(BF16)

    rows = rows_ref[...]
    part_ref[0] = dot(rows, gate_ref[0]).astype(BF16)
    part_ref[1] = dot(rows, up_ref[0]).astype(BF16)


def back_kernel(n, slots, width, step_cols, *refs):
    block_refs = refs[1 : 1 + n]
    pick_ref, scale_ref, down_ref = refs[1 + n : n + 4]
    scaled_ref, part_ref, rows_ref = refs[-3:]

    @pl.when(pl.program_id(0) == 0)
    def _():
        for b in range(n):
            pick = jnp.transpose(pick_ref[b].astype(F32))[:slots].astype(BF16)
            at = pl.ds(b * slots, slots)
            scale = scale_ref[at, :1]
            for left in range(0, width, step_cols):
                cols = slice(left, left + step_cols)
                picked = dot(pick, block_refs[b][0, :, cols])
                rows_ref[at, cols] = picked.astype(BF16)
                scaled_ref[at, cols] = (scale * picked).astype(BF16)

    part_ref[...] = dot(rows_ref[...], down_ref[0], ((1,), (1,))).astype(BF16)


def act_kernel(n_in, n_core, slots, units, width, tile, n_parts, *refs):
    me_ref = refs[0]
    fore_refs, back_refs = refs[1 : 1 + n_parts], refs[1 + n_parts : 1 + 2 * n_parts]
    pick_ref, scale_ref, gate_ref, up_ref = refs[1 + 2 * n_parts : 5 + 2 * n_parts]
    hidden_ref, dgate_ref, dup_ref = refs[-3 - n_core : -n_core]
    dense_refs = refs[-n_core:]
    step = pl.program_id(0)

    def scatter(b, values):
        pick_t = pick_ref[b][:, :slots]
        return dot(pick_t, values).astype(BF16)

    @pl.when(step == 0)
    def _():
        for b in range(n_in * n_core):
            at = pl.ds(b * slots, slots)
            total = jnp.zeros((slots, 1), F32)
            scale = scale_ref[at, :1]
            cut = tile_of(units, 256)
            for left in range(0, units, cut):
                cols = slice(left, left + cut)
                gate_sum = sum(f[0, at, cols].astype(F32) for f in fore_refs)
                up_sum = sum(f[1, at, cols].astype(F32) for f in fore_refs)
                back_sum = sum(f[at, cols].astype(F32) for f in back_refs)
                sig = jax.nn.sigmoid(gate_sum)
                silu = gate_sum * sig
                hidden = (silu * up_sum).astype(BF16)
                hidden_ref[at, cols] = hidden
                total = total + jnp.sum(hidden.astype(F32) * back_sum, axis=1, keepdims=True)
                q = scale * back_sum
                dgate_ref[at, cols] = (q * up_sum * sig * (1.0 + gate_sum * (1.0 - sig))).astype(BF16)
                dup_ref[at, cols] = (q * silu).astype(BF16)
            extra = dense_refs[0].shape[2] - width
            lane = lax.broadcasted_iota(jnp.int32, (slots, extra), 1)
            held = jnp.where(lane == me_ref[0], total, 0.0).astype(BF16)
            dense_refs[b % n_core][b // n_core, :, width:] = scatter(b, held)

    term = dot(dgate_ref[...], gate_ref[0], ((1,), (1,))) + dot(
        dup_ref[...], up_ref[0], ((1,), (1,))
    )
    term = term.astype(BF16)
    cols = pl.ds(pl.multiple_of(step * tile, LANES), tile)
    for b in range(n_in * n_core):
        dense_refs[b % n_core][b // n_core, :, cols] = scatter(
            b, term[b * slots : (b + 1) * slots]
        )


def body(tokens_in, out_grad, expert_ids, route_weight, gate_weight, up_weight, down_weight):
    token_count, top_count = expert_ids.shape
    experts_local, width, units = gate_weight.shape
    groups = lax.axis_size("dp")
    n_expert = lax.axis_size("expert")
    total_experts = experts_local * groups
    capacity = min(token_count, token_count * top_count * 5 // (4 * total_experts))
    slots = -(-capacity // 16) * 16
    n_out, n_in, n_core = split_dp(groups)
    me = lax.axis_index("dp")
    me_arr = me.astype(jnp.int32).reshape(1)
    sizes = (n_out, n_in, n_core)
    members = n_in * n_core
    rows = members * slots
    extra = LANES * (-(-total_experts // LANES))
    step_cols = tile_of(width, 512)

    def shift(x, axis, step, name):
        pairs = []
        for o in range(n_out):
            for i in range(n_in):
                for c in range(n_core):
                    at = [o, i, c]
                    dst = (o * n_in + i) * n_core + c
                    at[axis] = (at[axis] + step) % sizes[axis]
                    src = (at[0] * n_in + at[1]) * n_core + at[2]
                    pairs.append((src, dst))
        with jax.named_scope(name):
            return lax.ppermute(x, "dp", pairs)

    def source(r, i, c):
        at = (me // (n_in * n_core) + r) % n_out, (me // n_core + i) % n_in, (me + c) % n_core
        return ((at[0] * n_in + at[1]) * n_core + at[2]).astype(jnp.int32)

    near = sorted(range(n_out), key=lambda r: (min(r, n_out - r), r))
    far = near[::-1]

    def exchange(part, name):
        parts = [part]
        for step in range(1, n_expert):
            pairs = [((k + step) % n_expert, k) for k in range(n_expert)]
            with jax.named_scope(name + "_x"):
                parts.append(lax.ppermute(part, "expert", pairs))
        return parts

    smem = pl.BlockSpec(memory_space=pltpu.SMEM)
    anywhere = pl.BlockSpec(memory_space=pl.ANY)

    def at_rows(r, cols):
        return pl.BlockSpec((rows, cols), lambda j: (r, 0))

    def call(kernel, name, grid, ins, in_specs, outs, out_specs, before, flops, scratch=()):
        aliases = {}
        if before is not None:
            for k, held in enumerate(before):
                aliases[len(ins)] = k
                ins = [*ins, held]
                in_specs = [*in_specs, anywhere]
        return pl.pallas_call(
            kernel,
            grid=(grid,),
            in_specs=in_specs,
            out_specs=out_specs,
            out_shape=outs,
            scratch_shapes=scratch,
            input_output_aliases=aliases,
            compiler_params=pltpu.CompilerParams(vmem_limit_bytes=VMEM_LIMIT),
            cost_estimate=cost(flops // 1000, 0),
            name=name,
        )(*ins)

    def sds(shape, dtype=BF16):
        return jax.ShapeDtypeStruct(shape, dtype)

    unit_tile = tile_of(units, 256)
    all_rows = n_out * rows

    def fore_call(r, blocks, before):
        def kernel(*refs):
            fore_kernel(members, slots, top_count, width, step_cols, *refs[: 3 + members], *refs[-4:])

        weight = pl.BlockSpec((1, width, unit_tile), lambda j: (0, 0, j))
        return call(
            kernel,
            f"fore{r}",
            units // unit_tile,
            [me_arr, *blocks, gate_weight, up_weight],
            [smem, *[whole(b.shape) for b in blocks], weight, weight],
            [
                sds((all_rows, width)),
                sds((2, rows, units)),
                sds((members, token_count, LANES)),
                sds((rows, LANES), F32),
            ],
            [
                at_rows(r, width),
                pl.BlockSpec((2, rows, unit_tile), lambda j: (0, 0, j)),
                whole((members, token_count, LANES)),
                whole((rows, LANES)),
            ],
            before,
            2 * rows * width * 2 * units,
        )

    def back_call(r, grads, pick, scale, before):
        def kernel(*refs):
            back_kernel(members, slots, width, step_cols, *refs[: 4 + members], *refs[-3:])

        places = jnp.stack([source(r, i, c) for i in range(n_in) for c in range(n_core)])
        ins = [places, *[grads] * members, pick, scale, down_weight]
        in_specs = [
            pl.BlockSpec((1, token_count, width), lambda j, at, b=b: (at[b], 0, 0))
            for b in range(members)
        ]
        in_specs += [
            whole(pick.shape),
            whole(scale.shape),
            pl.BlockSpec((1, unit_tile, width), lambda j, at: (0, j, 0)),
        ]
        aliases = {}
        if before is not None:
            aliases[len(ins)] = 0
            ins.append(before[0])
            in_specs.append(anywhere)
        return pl.pallas_call(
            kernel,
            grid_spec=pltpu.PrefetchScalarGridSpec(
                num_scalar_prefetch=1,
                grid=(units // unit_tile,),
                in_specs=in_specs,
                out_specs=[
                    pl.BlockSpec((rows, width), lambda j, at: (r, 0)),
                    pl.BlockSpec((rows, unit_tile), lambda j, at: (0, j)),
                ],
                scratch_shapes=[pltpu.VMEM((rows, width), BF16)],
            ),
            out_shape=[sds((all_rows, width)), sds((rows, units))],
            input_output_aliases=aliases,
            compiler_params=pltpu.CompilerParams(vmem_limit_bytes=VMEM_LIMIT),
            cost_estimate=cost(2 * rows * width * units // 1000, 0),
            name=f"back{r}",
        )(*ins)

    def act_call(r, fore, back, pick, scale, before):
        tile = step_cols

        def kernel(*refs):
            act_kernel(
                n_in, n_core, slots, units, width, tile, n_expert,
                *refs[: 5 + 2 * n_expert], *refs[-3 - n_core :],
            )

        weight = pl.BlockSpec((1, tile, units), lambda j: (0, j, 0))
        dense = (n_in, token_count, width + extra)
        return call(
            kernel,
            f"act{r}",
            width // tile,
            [me_arr, *fore, *back, pick, scale, gate_weight, up_weight],
            [
                smem,
                *[whole(x.shape) for x in (*fore, *back, pick, scale)],
                weight,
                weight,
            ],
            [*[sds((all_rows, units))] * 3, *[sds(dense)] * n_core],
            [*[at_rows(r, units)] * 3, *[whole(dense)] * n_core],
            before,
            2 * rows * width * 2 * units,
        )

    meta = jnp.concatenate([expert_ids.astype(BF16), route_weight], axis=1)
    meta = jnp.pad(meta, ((0, 0), (0, LANES - meta.shape[1])))
    tokens = jnp.concatenate([tokens_in, meta], axis=1)

    rest = near[1:]
    turn = rest[::-1] + [0]
    fore, back, pick, scale, sums, lines_of = {}, {}, {}, {}, {}, {}
    hold = {"fore": None, "back": None, "act": None}
    y_done = []

    def done(kind):
        return hold[kind][0]

    def run_lines(r, block, after):
        lines = [block]
        for i in range(1, n_in):
            x = gate(block, (*after, *y_done[-1:]))
            y_done.append(shift(x, 1, i, f"tok{r}_y"))
            lines.append(y_done[-1])
        return lines

    def run_fore(r, lines, *after):
        blocks = []
        for line in lines:
            blocks.append(line)
            for c in range(1, n_core):
                blocks.append(shift(line, 2, c, f"tok{r}_core"))
        blocks[0] = gate(blocks[0], after)
        rows_in, part, pick[r], scale[r] = fore_call(r, blocks, hold["fore"])
        hold["fore"] = [rows_in]
        fore[r] = exchange(part, f"fore{r}")

    def run_back(r, *after):
        rows_back, part = back_call(r, gate(grads, after), pick[r], scale[r], hold["back"])
        hold["back"] = [rows_back]
        back[r] = exchange(part, f"back{r}")

    def run_act(r, *after):
        came = [gate(back[r][0], after), *back[r][1:]]
        hidden, dgate, dup, *dense = act_call(r, fore[r], came, pick[r], scale[r], hold["act"])
        hold["act"] = [hidden, dgate, dup]
        came = [shift(dense[c], 2, -c, f"sum{r}_core") for c in range(1, n_core)]
        lines_of[r] = [
            sum([x[i].astype(F32) for x in came], dense[0][i].astype(F32)).astype(BF16)
            for i in range(n_in)
        ]

    def run_sum(r, acted, came, before):
        after = tuple(x for x in (came, before) if x is not None)
        total = gate(lines_of[r][0], acted).astype(F32)
        for i in range(1, n_in):
            total = total + shift(gate(lines_of[r][i], after), 1, -i, f"sum{r}_y").astype(F32)
        sums[r] = total = total.astype(BF16)
        if r:
            sums[r] = shift(total, 0, -r, f"sum{r}_z")
        return total

    block = {0: tokens}
    for k, r in enumerate(rest):
        block[r] = shift(gate(tokens, block[rest[k - 2]] if k >= 2 else None), 0, r, f"tok{r}_z")
    grads = lax.all_gather(gate(out_grad, None), "dp", axis=0)
    lines = {0: run_lines(0, tokens, ())}
    for k, r in enumerate(near):
        if k + 1 < n_out:
            lines[near[k + 1]] = run_lines(near[k + 1], block[near[k + 1]], ())
        run_fore(r, lines[r])
        before = (done("fore"), *([fore[near[k - 1]][-1]] if k else []))
        if k + 1 < n_out:
            nxt = near[k + 1]
            lines[nxt] = [gate(line, before) for line in lines[nxt]]
        if k + 2 < n_out:
            nxt = near[k + 2]
            block[nxt] = gate(block[nxt], done("fore"))
    for k, r in enumerate(turn):
        run_back(r, done("fore"), *([fore[near[-1]][-1]] if k else [fore[near[-2]][-1]]))
    total = None
    for k, r in enumerate(turn):
        run_act(r, done("back"), *([] if k == 0 else [lines_of[turn[k - 1]][-1]]))
        if k:
            total = run_sum(turn[k - 1], done("act"), back[r][-1], total)
    run_sum(turn[-1], None, None, total)
    rows_in, rows_back = hold["fore"][0], hold["back"][0]
    hidden, dgate, dup = hold["act"]
    full = sum(sums[r].astype(F32) for r in near)
    input_grad = full[:, :width].astype(BF16)
    dots_of = full[:, width : width + total_experts]
    named = expert_ids[:, :, None] == jnp.arange(total_experts, dtype=jnp.int32)[None, None, :]
    weight_grad = jnp.sum(jnp.where(named, dots_of[:, None, :], 0.0), axis=2).astype(BF16)

    gate_grad = dot(rows_in, dgate, ((0,), (0,))).astype(BF16)
    up_grad = dot(rows_in, dup, ((0,), (0,))).astype(BF16)
    down_grad = dot(hidden, rows_back, ((0,), (0,))).astype(BF16)
    return (input_grad, weight_grad, gate_grad[None], up_grad[None], down_grad[None])


def solution(mesh):
    in_specs = (
        P("dp", "expert"),
        P("dp", "expert"),
        P("dp", None),
        P("dp", None),
        P("dp", "expert", None),
        P("dp", "expert", None),
        P("dp", None, "expert"),
    )
    out_specs = (
        P("dp", "expert"),
        P("dp", None),
        P("dp", "expert", None),
        P("dp", "expert", None),
        P("dp", None, "expert"),
    )
    return jax.shard_map(body, mesh=mesh, in_specs=in_specs, out_specs=out_specs, check_vma=False)
```

```python
import functools

import jax
import jax.numpy as jnp
from jax import lax
from jax.experimental import pallas as pl
from jax.experimental.pallas import tpu as pltpu
from jax.sharding import PartitionSpec as P

BF16 = jnp.bfloat16
F32 = jnp.float32
LANES = 128
VMEM_LIMIT = 44 * 1024 * 1024


def split_dp(size):
    core = 2 if size % 2 == 0 else 1
    chips = size // core
    inner = 1
    while chips % (inner * 2) == 0 and (inner * 2) * (inner * 2) <= chips:
        inner *= 2
    return chips // inner, inner, core


def tile_of(size, most):
    best = LANES
    for tile in range(LANES, most + 1, LANES):
        if size % tile == 0:
            best = tile
    return best


def dot(a, b, dims=((1,), (0,))):
    return lax.dot_general(a, b, (dims, ((), ())), preferred_element_type=F32)


def cost(flops, moved):
    return pl.CostEstimate(flops=flops, bytes_accessed=moved, transcendentals=0)


def gate(x, after):
    return x if after is None or (isinstance(after, tuple) and not after) else lax.optimization_barrier((x, after))[0]


def whole(shape):
    zeros = (0,) * len(shape)
    return pl.BlockSpec(shape, lambda *_: zeros)


def choose(pick_t, block_ref, cols, slots):
    pick = jnp.transpose(pick_t.astype(F32))[:slots].astype(BF16)
    return dot(pick, block_ref[:, cols]).astype(BF16)


def fore_kernel(n, slots, top, width, step_cols, *refs):
    me_ref, block_refs = refs[1], refs[2 : 2 + n]
    gate_ref, up_ref = refs[2 + n : 4 + n]
    rows_ref, part_ref, pick_ref, scale_ref = refs[-4:]

    @pl.when(pl.program_id(0) == 0)
    def _():
        me = me_ref[0].astype(F32)
        count = block_refs[0].shape[1]
        lower = (
            lax.broadcasted_iota(jnp.int32, (count, count), 1)
            < lax.broadcasted_iota(jnp.int32, (count, count), 0)
        ).astype(BF16)
        lane = lax.broadcasted_iota(jnp.int32, (count, LANES), 1).astype(F32)
        for b in range(n):
            meta = block_refs[b][0, :, width : width + LANES].astype(F32)
            hit = (meta[:, :top] == me).astype(F32)
            chosen = jnp.max(hit, axis=1, keepdims=True)
            weight = jnp.sum(hit * meta[:, top : 2 * top], axis=1, keepdims=True)
            chosen = jnp.broadcast_to(chosen, (count, LANES))
            order = dot(lower, chosen.astype(BF16))
            pick_t = jnp.where((order == lane) & (chosen > 0.5), 1.0, 0.0)
            pick_ref[b] = pick_t.astype(BF16)
            pick = jnp.transpose(pick_t)[:slots].astype(BF16)
            at = pl.ds(b * slots, slots)
            scale_ref[at, :] = dot(pick, jnp.broadcast_to(weight, (count, LANES)).astype(BF16))
            for left in range(0, width, step_cols):
                cols = slice(left, left + step_cols)
                rows_ref[at, cols] = dot(pick, block_refs[b][0, :, cols]).astype(BF16)

    rows = rows_ref[...]
    part_ref[0] = dot(rows, gate_ref[0]).astype(BF16)
    part_ref[1] = dot(rows, up_ref[0]).astype(BF16)


def back_kernel(n, slots, width, step_cols, *refs):
    block_refs = refs[1 : 1 + n]
    pick_ref, scale_ref, down_ref = refs[1 + n : n + 4]
    scaled_ref, part_ref, rows_ref = refs[-3:]

    @pl.when(pl.program_id(0) == 0)
    def _():
        for b in range(n):
            pick = jnp.transpose(pick_ref[b].astype(F32))[:slots].astype(BF16)
            at = pl.ds(b * slots, slots)
            scale = scale_ref[at, :1]
            for left in range(0, width, step_cols):
                cols = slice(left, left + step_cols)
                picked = dot(pick, block_refs[b][0, :, cols])
                rows_ref[at, cols] = picked.astype(BF16)
                scaled_ref[at, cols] = (scale * picked).astype(BF16)

    part_ref[...] = dot(rows_ref[...], down_ref[0], ((1,), (1,))).astype(BF16)


def act_kernel(n_in, n_core, slots, units, width, tile, n_parts, *refs):
    me_ref = refs[0]
    fore_refs, back_refs = refs[1 : 1 + n_parts], refs[1 + n_parts : 1 + 2 * n_parts]
    pick_ref, scale_ref, gate_ref, up_ref = refs[1 + 2 * n_parts : 5 + 2 * n_parts]
    hidden_ref, dgate_ref, dup_ref = refs[-3 - n_core : -n_core]
    dense_refs = refs[-n_core:]
    step = pl.program_id(0)

    def scatter(b, values):
        pick_t = pick_ref[b][:, :slots]
        return dot(pick_t, values).astype(BF16)

    @pl.when(step == 0)
    def _():
        for b in range(n_in * n_core):
            at = pl.ds(b * slots, slots)
            total = jnp.zeros((slots, 1), F32)
            scale = scale_ref[at, :1]
            cut = tile_of(units, 256)
            for left in range(0, units, cut):
                cols = slice(left, left + cut)
                gate_sum = sum(f[0, at, cols].astype(F32) for f in fore_refs)
                up_sum = sum(f[1, at, cols].astype(F32) for f in fore_refs)
                back_sum = sum(f[at, cols].astype(F32) for f in back_refs)
                sig = jax.nn.sigmoid(gate_sum)
                silu = gate_sum * sig
                hidden = (silu * up_sum).astype(BF16)
                hidden_ref[at, cols] = hidden
                total = total + jnp.sum(hidden.astype(F32) * back_sum, axis=1, keepdims=True)
                q = scale * back_sum
                dgate_ref[at, cols] = (q * up_sum * sig * (1.0 + gate_sum * (1.0 - sig))).astype(BF16)
                dup_ref[at, cols] = (q * silu).astype(BF16)
            extra = dense_refs[0].shape[2] - width
            lane = lax.broadcasted_iota(jnp.int32, (slots, extra), 1)
            held = jnp.where(lane == me_ref[0], total, 0.0).astype(BF16)
            dense_refs[b % n_core][b // n_core, :, width:] = scatter(b, held)

    term = dot(dgate_ref[...], gate_ref[0], ((1,), (1,))) + dot(
        dup_ref[...], up_ref[0], ((1,), (1,))
    )
    term = term.astype(BF16)
    cols = pl.ds(pl.multiple_of(step * tile, LANES), tile)
    for b in range(n_in * n_core):
        dense_refs[b % n_core][b // n_core, :, cols] = scatter(
            b, term[b * slots : (b + 1) * slots]
        )


def body(tokens_in, out_grad, expert_ids, route_weight, gate_weight, up_weight, down_weight):
    token_count, top_count = expert_ids.shape
    experts_local, width, units = gate_weight.shape
    groups = lax.axis_size("dp")
    n_expert = lax.axis_size("expert")
    total_experts = experts_local * groups
    capacity = min(token_count, token_count * top_count * 5 // (4 * total_experts))
    slots = -(-capacity // 16) * 16
    n_out, n_in, n_core = split_dp(groups)
    me = lax.axis_index("dp")
    me_arr = me.astype(jnp.int32).reshape(1)
    place = (me // (n_in * n_core), (me // n_core) % n_in, me % n_core)
    sizes = (n_out, n_in, n_core)
    members = n_in * n_core
    rows = members * slots
    extra = LANES * (-(-total_experts // LANES))
    step_cols = tile_of(width, 512)

    def shift(x, axis, step, name):
        pairs = []
        for o in range(n_out):
            for i in range(n_in):
                for c in range(n_core):
                    at = [o, i, c]
                    dst = (o * n_in + i) * n_core + c
                    at[axis] = (at[axis] + step) % sizes[axis]
                    src = (at[0] * n_in + at[1]) * n_core + at[2]
                    pairs.append((src, dst))
        with jax.named_scope(name):
            return lax.ppermute(x, "dp", pairs)

    def source(r, i, c):
        at = (me // (n_in * n_core) + r) % n_out, (me // n_core + i) % n_in, (me + c) % n_core
        return ((at[0] * n_in + at[1]) * n_core + at[2]).astype(jnp.int32)

    near = [0] + sorted(range(1, n_out), key=lambda r: (-min(r, n_out - r), r))
    far = near[::-1]

    def exchange(part, name):
        parts = [part]
        for step in range(1, n_expert):
            pairs = [((k + step) % n_expert, k) for k in range(n_expert)]
            with jax.named_scope(name + "_x"):
                parts.append(lax.ppermute(part, "expert", pairs))
        return parts

    smem = pl.BlockSpec(memory_space=pltpu.SMEM)
    anywhere = pl.BlockSpec(memory_space=pl.ANY)

    def at_rows(r, cols):
        return pl.BlockSpec((rows, cols), lambda j: (r, 0))

    def call(kernel, name, grid, ins, in_specs, outs, out_specs, before, flops, scratch=()):
        aliases = {}
        if before is not None:
            for k, held in enumerate(before):
                aliases[len(ins)] = k
                ins = [*ins, held]
                in_specs = [*in_specs, anywhere]
        return pl.pallas_call(
            kernel,
            grid=(grid,),
            in_specs=in_specs,
            out_specs=out_specs,
            out_shape=outs,
            scratch_shapes=scratch,
            input_output_aliases=aliases,
            compiler_params=pltpu.CompilerParams(vmem_limit_bytes=VMEM_LIMIT),
            cost_estimate=cost(flops // 1000, 0),
            name=name,
        )(*ins)

    def sds(shape, dtype=BF16):
        return jax.ShapeDtypeStruct(shape, dtype)

    unit_tile = tile_of(units, 256)
    all_rows = n_out * rows

    def fore_call(r, blocks, places, before):
        def kernel(*refs):
            fore_kernel(members, slots, top_count, width, step_cols, *refs[: 4 + members], *refs[-4:])

        ins = [jnp.stack(places), me_arr, *blocks, gate_weight, up_weight]
        in_specs = [smem]
        in_specs += [
            pl.BlockSpec((1, *blocks[b].shape[1:]), lambda j, at, b=b: (at[b], 0, 0))
            for b in range(members)
        ]
        in_specs += [pl.BlockSpec((1, width, unit_tile), lambda j, at: (0, 0, j))] * 2
        aliases = {}
        if before is not None:
            aliases[len(ins)] = 0
            ins.append(before[0])
            in_specs.append(anywhere)
        return pl.pallas_call(
            kernel,
            grid_spec=pltpu.PrefetchScalarGridSpec(
                num_scalar_prefetch=1,
                grid=(units // unit_tile,),
                in_specs=in_specs,
                out_specs=[
                    pl.BlockSpec((rows, width), lambda j, at: (r, 0)),
                    pl.BlockSpec((2, rows, unit_tile), lambda j, at: (0, 0, j)),
                    whole((members, token_count, LANES)),
                    whole((rows, LANES)),
                ],
            ),
            out_shape=[
                sds((all_rows, width)),
                sds((2, rows, units)),
                sds((members, token_count, LANES)),
                sds((rows, LANES), F32),
            ],
            input_output_aliases=aliases,
            compiler_params=pltpu.CompilerParams(vmem_limit_bytes=VMEM_LIMIT),
            cost_estimate=cost(4 * rows * width * units // 1000, 0),
            name=f"fore{r}",
        )(*ins)

    def back_call(r, grads, pick, scale, before):
        def kernel(*refs):
            back_kernel(members, slots, width, step_cols, *refs[: 4 + members], *refs[-3:])

        places = jnp.stack([source(r, i, c) for i in range(n_in) for c in range(n_core)])
        ins = [places, *[grads] * members, pick, scale, down_weight]
        in_specs = [
            pl.BlockSpec((1, token_count, width), lambda j, at, b=b: (at[b], 0, 0))
            for b in range(members)
        ]
        in_specs += [
            whole(pick.shape),
            whole(scale.shape),
            pl.BlockSpec((1, unit_tile, width), lambda j, at: (0, j, 0)),
        ]
        aliases = {}
        if before is not None:
            aliases[len(ins)] = 0
            ins.append(before[0])
            in_specs.append(anywhere)
        return pl.pallas_call(
            kernel,
            grid_spec=pltpu.PrefetchScalarGridSpec(
                num_scalar_prefetch=1,
                grid=(units // unit_tile,),
                in_specs=in_specs,
                out_specs=[
                    pl.BlockSpec((rows, width), lambda j, at: (r, 0)),
                    pl.BlockSpec((rows, unit_tile), lambda j, at: (0, j)),
                ],
                scratch_shapes=[pltpu.VMEM((rows, width), BF16)],
            ),
            out_shape=[sds((all_rows, width)), sds((rows, units))],
            input_output_aliases=aliases,
            compiler_params=pltpu.CompilerParams(vmem_limit_bytes=VMEM_LIMIT),
            cost_estimate=cost(2 * rows * width * units // 1000, 0),
            name=f"back{r}",
        )(*ins)

    def act_call(r, me_arr, fore, back, pick, scale, before):
        tile = step_cols

        def kernel(*refs):
            act_kernel(
                n_in, n_core, slots, units, width, tile, n_expert,
                *refs[: 5 + 2 * n_expert], *refs[-3 - n_core :],
            )

        weight = pl.BlockSpec((1, tile, units), lambda j: (0, j, 0))
        dense = (n_in, token_count, width + extra)
        return call(
            kernel,
            f"act{r}",
            width // tile,
            [me_arr, *fore, *back, pick, scale, gate_weight, up_weight],
            [
                smem,
                *[whole(x.shape) for x in (*fore, *back, pick, scale)],
                weight,
                weight,
            ],
            [*[sds((all_rows, units))] * 3, *[sds(dense)] * n_core],
            [*[at_rows(r, units)] * 3, *[whole(dense)] * n_core],
            before,
            2 * rows * width * 2 * units,
        )

    meta = jnp.concatenate([expert_ids.astype(BF16), route_weight], axis=1)
    meta = jnp.pad(meta, ((0, 0), (0, LANES - meta.shape[1])))
    tokens = jnp.concatenate([tokens_in, meta], axis=1)

    far = near[1:]
    turn = far + [0]
    fore, back, pick, scale = {}, {}, {}, {}
    dense, line, total, sums = {}, {}, {}, {}
    hold = {"fore": None, "back": None, "act": None}

    def run_fore(r, blocks, places):
        rows_in, part, pick[r], scale[r] = fore_call(r, blocks, places, hold["fore"])
        hold["fore"] = [rows_in]
        fore[r] = exchange(part, f"fore{r}")

    def run_back(r, *after):
        rows_back, part = back_call(r, gate(grads, after), pick[r], scale[r], hold["back"])
        hold["back"] = [rows_back]
        back[r] = exchange(part, f"back{r}")

    def run_act(r, me_now, *after):
        came = [gate(back[r][0], after), *back[r][1:]]
        out = act_call(r, me_now, fore[r], came, pick[r], scale[r], hold["act"])
        hold["act"], dense[r] = out[:3], out[3:]

    def sum_core(r, *after):
        came = [shift(gate(dense[r][c], after), 2, -c, f"sum{r}_core") for c in range(1, n_core)]
        line[r] = [
            sum([x[i].astype(F32) for x in came], dense[r][0][i].astype(F32)).astype(BF16)
            for i in range(n_in)
        ]

    def sum_in(r, *after):
        held = gate(line[r][0], after).astype(F32)
        for i in range(1, n_in):
            held = held + shift(line[r][i], 1, -i, f"sum{r}_y").astype(F32)
        total[r] = held.astype(BF16)
        pieces = [total[r]]
        if min(r, n_out - r) >= 2:
            half = LANES * ((width + extra) // LANES // 2)
            pieces = [total[r][:, half:], total[r][:, :half]]
        if r:
            pieces = [shift(x, 0, -r, f"sum{r}_z") for x in pieces]
        sums[r] = pieces

    tokens_all = lax.all_gather(tokens, "dp", axis=0)
    grads = lax.all_gather(gate(out_grad, tokens_all), "dp", axis=0)
    for r in turn:
        places = [source(r, i, c) for i in range(n_in) for c in range(n_core)]
        run_fore(r, [tokens_all] * members, places)
    run_back(turn[0], hold["fore"][0], *[fore[r][-1] for r in turn[:-1]])
    for r in turn[1:3]:
        run_back(r)
    first = back[turn[0]][-1]
    there = shift(gate(me_arr, (first, hold["back"][0])), 2, 1, "tick")
    me_now = there - (place[2] + 1) % n_core + place[2]
    for k, r in enumerate(turn):
        run_act(r, me_now, *([line[turn[k - 1]][0]] if k else []))
        if k:
            sum_in(turn[k - 1], dense[r][0])
        if 3 <= k + 2 < n_out:
            run_back(turn[k + 2], dense[r][0])
        after = [back[turn[k + 1]][-1]] if k + 1 < n_out else []
        if k >= 1:
            after.append(total[turn[k - 1]])
        if k >= 2:
            after.append(sums[turn[0]][min(k - 2, len(sums[turn[0]]) - 1)])
        if k == min(0, n_out - 2):
            after.append(fore[turn[-1]][-1])
        sum_core(r, *after)
    sum_in(turn[-1])
    full = sum(jnp.concatenate(sums[r][::-1], axis=1).astype(F32) for r in near)
    input_grad = full[:, :width].astype(BF16)
    dots_of = full[:, width : width + total_experts]
    named = expert_ids[:, :, None] == jnp.arange(total_experts, dtype=jnp.int32)[None, None, :]
    weight_grad = jnp.sum(jnp.where(named, dots_of[:, None, :], 0.0), axis=2).astype(BF16)

    rows_in, rows_back = hold["fore"][0], hold["back"][0]
    hidden, dgate, dup = hold["act"]
    full = sum(jnp.concatenate(sums[r][::-1], axis=1).astype(F32) for r in near)
    input_grad = full[:, :width].astype(BF16)
    dots_of = full[:, width : width + total_experts]
    named = expert_ids[:, :, None] == jnp.arange(total_experts, dtype=jnp.int32)[None, None, :]
    weight_grad = jnp.sum(jnp.where(named, dots_of[:, None, :], 0.0), axis=2).astype(BF16)

    gate_grad = dot(rows_in, dgate, ((0,), (0,))).astype(BF16)
    up_grad = dot(rows_in, dup, ((0,), (0,))).astype(BF16)
    down_grad = dot(hidden, rows_back, ((0,), (0,))).astype(BF16)
    return (input_grad, weight_grad, gate_grad[None], up_grad[None], down_grad[None])


def solution(mesh):
    in_specs = (
        P("dp", "expert"),
        P("dp", "expert"),
        P("dp", None),
        P("dp", None),
        P("dp", "expert", None),
        P("dp", "expert", None),
        P("dp", None, "expert"),
    )
    out_specs = (
        P("dp", "expert"),
        P("dp", None),
        P("dp", "expert", None),
        P("dp", "expert", None),
        P("dp", None, "expert"),
    )
    return jax.shard_map(body, mesh=mesh, in_specs=in_specs, out_specs=out_specs, check_vma=False)
```
